32 devices in a mesh: rep: 2 (over y), ctx: 4 (over z), smp: 4 (over x, core).
Axes of the slice: x: 2, y: 2, z: 4, core: 2. Of those that a mesh axis runs over, the one named last changes fastest.
Arguments:
- kv: bfloat16 [65536, 576], P(('rep', 'ctx')), parts along dimension 0
- idx_key: bfloat16 [65536, 128], P(('rep', 'ctx')), parts along dimension 0
- query: bfloat16 [16, 64, 128, 576], P(('rep', 'smp'), None, 'ctx'), parts along dimension 0
- dout: bfloat16 [16, 64, 128, 512], P(('rep', 'smp'), None, 'ctx'), parts along dimension 0, may hold values from -48 to 48
- idx_query: bfloat16 [16, 64, 64, 128], P(('rep', 'smp'), None, 'ctx'), parts along dimension 0
- idx_weight: bfloat16 [16, 64, 64], P(('rep', 'smp'), None, 'ctx'), parts along dimension 0, may hold values from 0.099609375 to 1
- blocks: int32 [16, 16], P(('rep', 'smp')), parts along dimension 0, may hold values from 0 to 511, as said below
- counts: int32 [16], P(('rep', 'smp')), parts along dimension 0, may hold values from 8 to 16, as said below
Outputs:
- d_query: bfloat16 [16, 64, 128, 576], P(('rep', 'smp'), None, 'ctx'), parts along dimension 0
- d_idx_query: bfloat16 [16, 64, 64, 128], P(('rep', 'smp'), None, 'ctx'), parts along dimension 0
- d_idx_weight: bfloat16 [16, 64, 64], P(('rep', 'smp'), None, 'ctx'), parts along dimension 0
- d_kv: bfloat16 [65536, 576], P(('rep', 'ctx', 'smp')), parts along dimension 0
- d_idx_key: bfloat16 [65536, 128], P(('rep', 'ctx', 'smp')), parts along dimension 0
The draws below stay inside these ranges and needn't reach their ends.
There are 2 independent parts, one for each index of `rep`. The reference program is written for one: setup_inputs(seed, part) draws one part's arguments, and reference() takes and returns one part's arrays. A program takes and returns all parts, laid end to end along the dimension named above; each array names one. Nothing has to cross between parts.
Inputs may be any that keep to these rules, and one draw needn't show every extreme that they name: The first counts[s] entries of blocks[s] are distinct and ascending, the rest are 0. Of one sample's selected blocks at most 8 lie in one shard of 8192 prompt tokens, and for every sample some shard holds exactly 8. `counts`: sample 0 of every prompt has 16.
All inputs are finite; a program needn't handle non-finite values.
Results may differ from the reference program's by a relative error of at most 0.005.
Values may be sent and summed in bfloat16 or wider, within the bound.
No kernel may reach another device: no remote copies, remote signals or barrier semaphores. Data moves between devices by JAX's collectives and lax.ppermute only.
A program may use at most 256 MiB of HBM per device.

```python
import math
import jax
import jax.numpy as jnp
from jax import lax

DL = 512
DK = 576
DI = 128
H = 128
HI = 64
BLK = 64
MAXB = 16
SAMPLES = 8
QS = 64
CTX = 32768
CTX_DEV = 8192
CAP = 8
N_CTX = 4


def latent_table(key):
    return jax.random.normal(jax.random.fold_in(key, 101), (CTX, DK), jnp.float32)


def index_table(key):
    return jax.random.normal(jax.random.fold_in(key, 102), (CTX, DI), jnp.float32)


def sample_blocks(key, number):
    nblk = CTX // BLK
    blocks_per_shard = CTX_DEV // BLK
    first, runner_index, third = jax.random.split(key, 3)
    spread_top = max(2 ** 24 // nblk, 1)
    random_jitter = jax.random.randint(first, (nblk,), 0, spread_top) * nblk + jnp.arange(nblk, dtype=jnp.int32)
    grid = random_jitter.reshape(N_CTX, blocks_per_shard)
    placing = jnp.argsort(jnp.argsort(-grid, axis=1), axis=1)
    allowed_mask = (placing < CAP).reshape(-1)
    extra_credit = jax.random.randint(runner_index, (N_CTX,), 0, 4)
    busiest_block = jax.random.randint(third, (), 0, N_CTX)
    extra_credit = jnp.where(jnp.arange(N_CTX) == busiest_block, 8, extra_credit)
    rank_score = jnp.where(allowed_mask, (jnp.repeat(extra_credit, blocks_per_shard) + 1) * 2 ** 24 + random_jitter, random_jitter)
    chosen = jnp.argsort(-rank_score)[:MAXB].astype(jnp.int32)
    place = jnp.arange(MAXB, dtype=jnp.int32)
    keyed = jnp.sort(jnp.where(place < number, chosen, nblk + place))
    return jnp.where(keyed < nblk, keyed, 0).astype(jnp.int32)


def block_lists(key):
    base = jax.random.fold_in(key, 103)
    counts = MAXB - jax.random.randint(jax.random.fold_in(base, 7), (SAMPLES,), 0, 9)
    counts = counts.at[0].set(MAXB).astype(jnp.int32)
    key_rows = jax.random.split(base, SAMPLES)
    blocks = jax.vmap(sample_blocks)(key_rows, counts)
    return (blocks, counts)


def draw_kv(key, part):
    table = latent_table(key)
    return table.astype(jnp.bfloat16)


def draw_idx_key(key, part):
    table = index_table(key)
    return table.astype(jnp.bfloat16)


def draw_query(key, part):
    key = jax.random.fold_in(key, 3)
    base = jax.random.normal(key, (SAMPLES, QS, H, DK), jnp.float32)
    return base.astype(jnp.bfloat16)


def draw_idx_query(key, part):
    key = jax.random.fold_in(key, 4)
    base = jax.random.normal(key, (SAMPLES, QS, HI, DI), jnp.float32)
    return base.astype(jnp.bfloat16)


def draw_blocks(key, part):
    blocks, counts = block_lists(key)
    return blocks


def draw_counts(key, part):
    blocks, counts = block_lists(key)
    return counts


def level_of(stream_key, shape, cuts, smallest, high):
    factor_of = 1.0
    for axis_at, blocks in cuts:
        draws = jax.random.uniform(jax.random.fold_in(jax.random.fold_in(stream_key, 6), axis_at), (blocks,), jnp.float32, smallest / len(cuts), high / len(cuts))
        factor_of = factor_of * jnp.repeat(jnp.exp(draws), shape[axis_at] // blocks).reshape((-1,) + (1,) * (len(shape) - 1 - axis_at))
    return factor_of


def centred(stream_key, extent, scale, reach, cuts=(), kind=jnp.bfloat16):
    values = scale * jax.random.normal(stream_key, extent, jnp.float32)
    if cuts:
        values = values * level_of(stream_key, extent, cuts, -0.22, 0.18)
    return jnp.clip(values, -reach, reach).astype(kind)


def setup_inputs(seed: int = 0, part: int = 0) -> dict:
    key_of = jax.random.split(jax.random.key(seed), 9)
    own_keys = jax.random.split(jax.random.fold_in(key_of[8], part), 9)
    kv = draw_kv(jax.random.fold_in(jax.random.fold_in(key_of[8], part), 71), part)
    idx_key = draw_idx_key(jax.random.fold_in(jax.random.fold_in(key_of[8], part), 71), part)
    query = draw_query(jax.random.fold_in(jax.random.fold_in(key_of[8], part), 71), part)
    dout = centred(own_keys[3], (SAMPLES, QS, H, DL), 8.0, 48.0, ((0, 4), (2, 4)))
    idx_query = draw_idx_query(jax.random.fold_in(jax.random.fold_in(key_of[8], part), 71), part)
    idx_weight = jnp.clip(jnp.exp(math.log(1.0) - 2.306499 * jax.random.uniform(own_keys[5], (SAMPLES, QS, HI), jnp.float32) ** level_of(own_keys[5], (SAMPLES, QS, HI), ((0, 4), (2, 4)), -0.2, 0.2)), 0.099609375, 1.0).astype(jnp.bfloat16)
    blocks = draw_blocks(jax.random.fold_in(jax.random.fold_in(key_of[8], part), 71), part)
    counts = draw_counts(jax.random.fold_in(jax.random.fold_in(key_of[8], part), 71), part)
    return {"kv": kv, "idx_key": idx_key, "query": query, "dout": dout, "idx_query": idx_query, "idx_weight": idx_weight, "blocks": blocks, "counts": counts}


SCALE = 192.0 ** (-0.5)
IDX_SCALE = 128.0 ** (-0.5)
LOSS = 256.0
NEG = -1e+30
UPPER_LIMIT = lax.Precision.HIGHEST

def forward_part(key_rows, ikeys, live_key, query, idx_query, idx_weight):
    sn, rn, hn, width = query.shape
    flat = query.reshape(sn, rn * hn, width).astype(jnp.float32)
    scores = jnp.einsum('sqd,snd->sqn', flat, key_rows.astype(jnp.float32), precision=UPPER_LIMIT) * SCALE
    scores = jnp.where(live_key[:, None, :], scores, NEG)
    peak = lax.optimization_barrier(jnp.max(scores, axis=-1, keepdims=True))
    expo = jnp.exp(scores - peak)
    probability_rows = expo / lax.optimization_barrier(jnp.sum(expo, axis=-1, keepdims=True))
    mass = lax.optimization_barrier(jnp.sum(probability_rows.reshape(sn, rn, hn, -1), axis=2))
    inner = jnp.einsum('srgd,snd->srgn', idx_query.astype(jnp.float32), ikeys.astype(jnp.float32), precision=UPPER_LIMIT) * IDX_SCALE
    logit = jnp.einsum('srg,srgn->srn', idx_weight.astype(jnp.float32), jnp.maximum(inner, 0.0), precision=UPPER_LIMIT)
    return (probability_rows, inner, mass, logit)

def kl_grad(mass, logit, live_key):
    target = mass / H
    masked = jnp.where(live_key[:, None, :], logit, NEG)
    peak = lax.optimization_barrier(jnp.max(masked, axis=-1, keepdims=True))
    expo = jnp.exp(masked - peak)
    share = expo / lax.optimization_barrier(jnp.sum(expo, axis=-1, keepdims=True))
    return LOSS * (share - target)

def backward_part(key_rows, ikeys, query, dout, idx_query, idx_weight, probability_rows, inner, grad):
    sn, rn, hn, width = query.shape
    latent_state = dout.shape[-1]
    flat = query.reshape(sn, rn * hn, width).astype(jnp.float32)
    flat_gradient = dout.reshape(sn, rn * hn, latent_state).astype(jnp.float32)
    key_rows32 = key_rows.astype(jnp.float32)
    probability_gradient = jnp.einsum('vbf,vgf->vbg', flat_gradient, key_rows32[:, :, :latent_state], precision=UPPER_LIMIT)
    delta = lax.optimization_barrier(jnp.sum(probability_rows * probability_gradient, axis=-1, keepdims=True))
    dscore = lax.optimization_barrier((probability_rows * (probability_gradient - delta) * SCALE).astype(jnp.bfloat16)).astype(jnp.float32)
    dquery = jnp.einsum('sqn,snd->sqd', dscore, key_rows32, precision=UPPER_LIMIT).astype(jnp.bfloat16).reshape(sn, rn, hn, width)
    dkeys = jnp.einsum('sqn,sqd->snd', dscore, flat, precision=UPPER_LIMIT)
    rounded_count = lax.optimization_barrier(probability_rows.astype(jnp.bfloat16)).astype(jnp.float32)
    value_gradient = jnp.einsum('tjw,tjv->twv', rounded_count, flat_gradient, precision=UPPER_LIMIT)
    dkeys = dkeys.at[:, :, :latent_state].add(value_gradient)
    weight = idx_weight.astype(jnp.float32)
    edge = jnp.where(inner > 0.0, grad[:, :, None, :] * weight[:, :, :, None] * IDX_SCALE, 0.0)
    edge = lax.optimization_barrier(edge.astype(jnp.bfloat16)).astype(jnp.float32)
    dweight = jnp.einsum('srn,srgn->srg', grad, jnp.maximum(inner, 0.0), precision=UPPER_LIMIT).astype(jnp.bfloat16)
    didxq = jnp.einsum('srgn,snd->srgd', edge, ikeys.astype(jnp.float32), precision=UPPER_LIMIT).astype(jnp.bfloat16)
    didxk = jnp.einsum('srgn,srgd->snd', edge, idx_query.astype(jnp.float32), precision=UPPER_LIMIT)
    return (dquery, didxq, dweight, dkeys, didxk)

def reference(kv, idx_key, query, dout, idx_query, idx_weight, blocks, counts):
    offsets = jnp.arange(BLK, dtype=jnp.int32)
    places = jnp.arange(MAXB * BLK, dtype=jnp.int32) // BLK

    def one_sample(totals, inputs):
        qrow, drow, iqrow, wrow, listed, number = inputs
        tokens = (listed.astype(jnp.int32)[:, None] * BLK + offsets[None, :]).reshape(-1)
        key_rows = jnp.take(kv, tokens, axis=0)[None]
        ikeys = jnp.take(idx_key, tokens, axis=0)[None]
        live_key = (places < number)[None]
        probability_rows, inner, mass, logit = forward_part(key_rows, ikeys, live_key, qrow[None], iqrow[None], wrow[None])
        grad = kl_grad(mass, logit, live_key)
        dquery, didxq, dweight, dkeys, didxk = backward_part(key_rows, ikeys, qrow[None], drow[None], iqrow[None], wrow[None], probability_rows, inner, grad)
        joined = jnp.concatenate([dkeys[0], didxk[0]], axis=1)
        totals = totals.at[tokens].add(joined)
        return (totals, (dquery[0], didxq[0], dweight[0]))
    start = jnp.zeros((CTX, DK + DI), jnp.float32)
    totals, (d_query, d_idx_query, d_idx_weight) = lax.scan(one_sample, start, (query, dout, idx_query, idx_weight, blocks, counts))
    return (d_query, d_idx_query, d_idx_weight, totals[:, :DK].astype(jnp.bfloat16), totals[:, DK:].astype(jnp.bfloat16))
```

```python
import functools

import jax
import jax.numpy as jnp
from jax import lax
from jax.experimental import pallas as pl
from jax.experimental.pallas import tpu as pltpu
from jax.sharding import PartitionSpec as P

H = 128
BLK = 64
HALF = BLK // 2
LANE = 128

SCALE = 192.0 ** (-0.5)
IDX_SCALE = 128.0 ** (-0.5)
LOSS = 256.0
NEG = -1e30
EXACT = lax.Precision.HIGHEST
VMEM_BYTES = 56 * 1024 * 1024

NT = (((1,), (1,)), ((), ()))
F32 = jnp.float32
BF16 = jnp.bfloat16


def params():
    return pltpu.CompilerParams(vmem_limit_bytes=VMEM_BYTES)


def cost(flops, moved):
    return pl.CostEstimate(flops=int(flops), bytes_accessed=int(moved), transcendentals=0)


def any_spec():
    return pl.BlockSpec(memory_space=pl.ANY)


def vmem_spec():
    return pl.BlockSpec(memory_space=pltpu.VMEM)


def smem_spec():
    return pl.BlockSpec(memory_space=pltpu.SMEM)


def below(meta, base, listed, number, bound):
    total = jnp.int32(0)
    for i in range(listed):
        total += jnp.where((i < number) & (meta[base + i] < bound), 1, 0)
    return total


def span(meta, base, listed, number, shard, per_shard):
    first = below(meta, base, listed, number, shard * per_shard)
    last = below(meta, base, listed, number, (shard + 1) * per_shard)
    return first, last - first


def pack_kernel(dims, meta, kv, ik, *rest):
    samples, listed, slots, per_shard, width, tiles = dims
    outs, (kbuf, ibuf, sem) = rest[:samples], rest[samples:]
    me = meta[samples * (listed + 1)]
    copies = []
    for s in range(samples):
        number = meta[samples * listed + s]
        first, _ = span(meta, s * listed, listed, number, me, per_shard)
        for j in range(slots):
            place = jnp.minimum(first + j, listed - 1)
            block = jnp.clip(meta[s * listed + place] - me * per_shard, 0, per_shard - 1)
            rows = pl.ds(pl.multiple_of(block * BLK, BLK), BLK)
            at = s * slots + j
            one = pltpu.make_async_copy(kv.at[rows], kbuf.at[at], sem.at[at, 0])
            two = pltpu.make_async_copy(ik.at[rows], ibuf.at[at], sem.at[at, 1])
            one.start()
            two.start()
            copies.append((one, two))
    for s in range(samples):
        for j in range(slots):
            at = s * slots + j
            copies[at][0].wait()
            copies[at][1].wait()
            out = outs[s]
            for c in range(tiles):
                out[pl.ds((c * slots + j) * BLK, BLK), :] = kbuf[at, :, c * LANE : (c + 1) * LANE]
            out[pl.ds((tiles * slots + j) * BLK, BLK), :] = ibuf[at]
            tail = kbuf[at, :, tiles * LANE : width]
            out[pl.ds((tiles + 1) * slots * BLK + j * HALF, HALF), :] = jnp.concatenate(
                [tail[:HALF], tail[HALF:]], axis=1
            )


def pack(meta, kv, ik, dims):
    samples, listed, slots, per_shard, width, tiles = dims
    rows = slots * ((tiles + 1) * BLK + HALF)
    return pl.pallas_call(
        functools.partial(pack_kernel, dims),
        out_shape=[jax.ShapeDtypeStruct((rows, LANE), BF16)] * samples,
        in_specs=[smem_spec(), any_spec(), any_spec()],
        out_specs=[vmem_spec()] * samples,
        scratch_shapes=[
            pltpu.VMEM((samples * slots, BLK, width), BF16),
            pltpu.VMEM((samples * slots, BLK, ik.shape[1]), BF16),
            pltpu.SemaphoreType.DMA((samples * slots, 2)),
        ],
        compiler_params=params(),
        cost_estimate=cost(0, 4 * samples * rows * LANE * 2),
        name="pack",
    )(meta, kv, ik)


def attention_kernel(dims, s, n_ctx, heads, groups, tall, aliased, meta, *refs):
    samples, listed, slots, per_shard, width, tiles = dims
    near = 2 * n_ctx - 1
    q_ref, do_ref, iq_ref, wcol_ref = refs[:4]
    slabs = refs[4 : 4 + near]
    refs = refs[4 + near + (1 if aliased else 0) :]
    dq_ref, ikey_ref = refs[:2]
    outs = refs[2 : 2 + near]
    parts = refs[2 + near : 2 + near + n_ctx]
    k_scr, kt_scr, acc, mass_t, logits, shares = refs[2 + near + n_ctx :]
    step = pl.program_id(0)
    steps = pl.num_programs(0)
    value = tiles * LANE
    keys = listed * BLK
    rows = q_ref.shape[0]
    times = rows // heads
    me = meta[samples * (listed + 1)]
    number = meta[samples * listed + s]
    live = number * BLK

    def shard_of(at):
        if at == 0:
            return me
        return me - at if at < n_ctx else me + (at - n_ctx + 1)

    @pl.when(step == 0)
    def _():
        for at in range(near):
            slab = slabs[at]
            first, many = span(meta, s * listed, listed, number, shard_of(at), per_shard)

            def place(j, _, slab=slab, first=first):
                to = pl.multiple_of((first + j) * BLK, BLK)
                for c in range(tiles + 1):
                    piece = slab[pl.ds(pl.multiple_of((c * slots + j) * BLK, BLK), BLK), :]
                    if c < tiles:
                        k_scr[pl.ds(to, BLK), c * LANE : (c + 1) * LANE] = piece
                    else:
                        ikey_ref[pl.ds(to, BLK), :] = piece
                piece = slab[
                    pl.ds(pl.multiple_of((tiles + 1) * slots * BLK + j * HALF, HALF), HALF), :
                ]
                side = LANE // 2
                k_scr[pl.ds(to, HALF), value : value + side] = piece[:, :side]
                k_scr[pl.ds(pl.multiple_of(to + HALF, HALF), HALF), value : value + side] = piece[
                    :, side:
                ]
                return 0

            lax.fori_loop(0, many, place, 0)

        def clear(i, _):
            to = pl.multiple_of(i * BLK, BLK)
            k_scr[pl.ds(to, BLK), :] = jnp.zeros((BLK, k_scr.shape[1]), BF16)
            ikey_ref[pl.ds(to, BLK), :] = jnp.zeros((BLK, ikey_ref.shape[1]), BF16)
            return 0

        lax.fori_loop(number, listed, clear, 0)
        k_scr[:, width:] = jnp.zeros((keys, k_scr.shape[1] - width), BF16)
        kt_scr[...] = k_scr[...].T
        acc[...] = jnp.zeros_like(acc)
        mass_t[...] = jnp.zeros_like(mass_t)

    q = q_ref[...]
    do = do_ref[...]
    scores = lax.dot_general(k_scr[:, :width], q, NT, preferred_element_type=F32)
    alive = lax.broadcasted_iota(jnp.int32, (keys, 1), 0) < live
    scores = jnp.where(alive, scores * SCALE, NEG)
    expo = jnp.exp(scores - jnp.max(scores, axis=0, keepdims=True))
    probs = expo * (1.0 / jnp.sum(expo, axis=0, keepdims=True))
    probs_b = probs.astype(BF16)
    dprob = lax.dot_general(k_scr[:, :value], do, NT, preferred_element_type=F32)
    delta = jnp.sum(probs * dprob, axis=0, keepdims=True)
    dscore = (probs * (dprob - delta) * SCALE).astype(BF16)
    dq_t = jnp.dot(kt_scr[...], dscore, preferred_element_type=F32)
    dq_ref[...] = dq_t.T[:, :width].astype(BF16)
    acc[:, :width] += jnp.dot(dscore, q, preferred_element_type=F32)
    acc[:, :value] += jnp.dot(probs_b, do, preferred_element_type=F32)
    every = mass_t.shape[1]
    row = lax.broadcasted_iota(jnp.int32, (rows, every), 0) // heads + step * times
    column = lax.broadcasted_iota(jnp.int32, (rows, every), 1)
    member = jnp.where(row == column, 1.0, 0.0).astype(BF16)
    mass_t[...] += jnp.dot(probs_b, member, preferred_element_type=F32)

    inner = lax.dot_general(iq_ref[...], ikey_ref[...], NT, preferred_element_type=F32)
    weighed = jnp.maximum(inner, 0.0) * (wcol_ref[...] * IDX_SCALE)
    if groups % 8 == 0:
        logit = jnp.sum(weighed.reshape(times, groups, keys), axis=1)
    else:
        gather = (
            lax.broadcasted_iota(jnp.int32, (times, times * groups), 1) // groups
            == lax.broadcasted_iota(jnp.int32, (times, times * groups), 0)
        ).astype(F32)
        logit = jnp.dot(gather, weighed, precision=EXACT, preferred_element_type=F32)
    logits[pl.ds(pl.multiple_of(step * times, times), times), :] = logit

    @pl.when(step == steps - 1)
    def _():
        for at in range(near):
            out = outs[at]
            first, many = span(meta, s * listed, listed, number, shard_of(at), per_shard)

            def emit(j, _, out=out, first=first):
                rows = pl.ds(pl.multiple_of((first + j) * BLK, BLK), BLK)
                for c in range(tiles):
                    out[pl.ds(pl.multiple_of((c * slots + j) * BLK, BLK), BLK), :] = acc[
                        rows, c * LANE : (c + 1) * LANE
                    ].astype(BF16)
                tail = acc[rows, value : value + LANE // 2].astype(BF16)
                out[pl.ds(pl.multiple_of(tiles * slots * BLK + j * HALF, HALF), HALF), :] = (
                    jnp.concatenate([tail[:HALF], tail[HALF:]], axis=1)
                )
                return 0

            lax.fori_loop(0, many, emit, 0)
        mass = mass_t[...].T
        part = every // n_ctx
        for c in range(n_ctx):
            shares[c, :part] = mass[c * part : (c + 1) * part]
            shares[c, part:] = logits[c * part : (c + 1) * part, :]
        for k in range(n_ctx):
            parts[k][...] = shares[lax.rem(me + k, n_ctx)]


def attention(meta, query, dout, idx_query, wcol, slabs, d_query, dims, s, n_ctx, heads, tall):
    samples, listed, slots, per_shard, width, tiles = dims
    total = query.shape[1]
    every = total // heads
    groups = idx_query.shape[1] // every
    side = tall // heads * groups
    steps = total // tall
    value = tiles * LANE
    keys = listed * BLK
    wide = (width + LANE - 1) // LANE * LANE
    near = 2 * n_ctx - 1
    ind = idx_query.shape[2]
    aliased = d_query is not None
    grad_rows = slots * (tiles * BLK + HALF)
    part = every // n_ctx

    def row_spec(size, columns):
        return pl.BlockSpec((None, size, columns), lambda i: (s, i, 0))

    def whole(shape):
        return pl.BlockSpec(shape, lambda i: (0,) * len(shape))

    in_specs = [
        smem_spec(),
        row_spec(tall, width),
        row_spec(tall, value),
        row_spec(side, ind),
        row_spec(side, 1),
    ] + [whole(slabs[0].shape)] * near
    args = [meta, query, dout, idx_query, wcol] + slabs
    aliases = {}
    if aliased:
        in_specs.append(any_spec())
        aliases = {len(args): 0}
        args.append(d_query)
    out_shape = (
        [
            jax.ShapeDtypeStruct(query.shape, BF16),
            jax.ShapeDtypeStruct((keys, ind), BF16),
        ]
        + [jax.ShapeDtypeStruct((grad_rows, LANE), BF16)] * near
        + [jax.ShapeDtypeStruct((2 * part, keys), F32)] * n_ctx
    )
    out_specs = (
        [row_spec(tall, width), whole((keys, ind))]
        + [whole((grad_rows, LANE))] * near
        + [whole((2 * part, keys))] * n_ctx
    )
    flops = 2 * total * keys * (3 * width + 2 * value) + 2 * total // heads * groups * keys * ind
    out = pl.pallas_call(
        functools.partial(attention_kernel, dims, s, n_ctx, heads, groups, tall, aliased),
        grid=(steps,),
        out_shape=out_shape,
        in_specs=in_specs,
        out_specs=out_specs,
        scratch_shapes=[
            pltpu.VMEM((keys, wide), BF16),
            pltpu.VMEM((wide, keys), BF16),
            pltpu.VMEM((keys, wide), F32),
            pltpu.VMEM((keys, every), F32),
            pltpu.VMEM((every, keys), F32),
            pltpu.VMEM((n_ctx, 2 * part, keys), F32),
        ],
        input_output_aliases=aliases,
        compiler_params=params(),
        cost_estimate=cost(flops, total * (2 * width + value) * 2 + 14 * grad_rows * LANE * 2),
        name="attention",
    )(*args)
    return out[0], out[1], out[2 : 2 + near], out[2 + near :]


def divergence_kernel(samples, listed, n_ctx, meta, *refs):
    out = refs[-1]
    part, keys = out.shape[1:]
    for s in range(samples):
        total = refs[s * n_ctx][...]
        for k in range(1, n_ctx):
            total += refs[s * n_ctx + k][...]
        live = meta[samples * listed + s] * BLK
        alive = lax.broadcasted_iota(jnp.int32, (1, keys), 1) < live
        logit = jnp.where(alive, total[part:], NEG)
        expo = jnp.exp(logit - jnp.max(logit, axis=1, keepdims=True))
        share = expo / jnp.sum(expo, axis=1, keepdims=True)
        out[s] = LOSS * (share - total[:part] * (1.0 / H))


def divergence(meta, pieces, samples, listed, n_ctx):
    both, keys = pieces[0].shape
    return pl.pallas_call(
        functools.partial(divergence_kernel, samples, listed, n_ctx),
        out_shape=jax.ShapeDtypeStruct((samples, both // 2, keys), F32),
        in_specs=[smem_spec()] + [vmem_spec()] * len(pieces),
        out_specs=vmem_spec(),
        compiler_params=params(),
        cost_estimate=cost(0, len(pieces) * both * keys * 4),
        name="divergence",
    )(meta, *pieces)


def indexer_kernel(dims, n_ctx, groups, meta, *refs):
    samples, listed, slots, per_shard, width, tiles = dims
    near = 2 * n_ctx - 1
    iq_ref, wcol_ref = refs[:2]
    ikeys = refs[2 : 2 + samples]
    grads = refs[2 + samples : 2 + samples + n_ctx]
    refs = refs[2 + samples + n_ctx :]
    diq_ref, dw_ref = refs[:2]
    outs = refs[2 : 2 + near]
    whole, ik_scr, acc_t, acc = refs[2 + near :]
    s, c = pl.program_id(0), pl.program_id(1)
    me = meta[samples * (listed + 1)]
    part, keys = grads[0].shape[1:]

    @pl.when(c == 0)
    def _():
        for k in range(n_ctx):
            whole[lax.rem(me - k + n_ctx, n_ctx)] = grads[k][s]
        for at in range(samples):

            @pl.when(s == at)
            def _(at=at):
                ik_scr[...] = ikeys[at][...]

        acc_t[...] = jnp.zeros_like(acc_t)

    iq = iq_ref[...]
    inner = lax.dot_general(iq, ik_scr[...], NT, preferred_element_type=F32)
    grad = whole[c]
    if groups % 8 == 0:
        grad = jnp.broadcast_to(grad[:, None, :], (part, groups, keys)).reshape(part * groups, keys)
    else:
        expand = (
            lax.broadcasted_iota(jnp.int32, (part * groups, part), 0) // groups
            == lax.broadcasted_iota(jnp.int32, (part * groups, part), 1)
        ).astype(F32)
        grad = jnp.dot(expand, grad, precision=EXACT, preferred_element_type=F32)
    edge = jnp.where(inner > 0.0, grad * (wcol_ref[...] * IDX_SCALE), 0.0).astype(BF16)
    dw_ref[...] = jnp.sum(grad * jnp.maximum(inner, 0.0), axis=1, keepdims=True) * IDX_SCALE
    diq_ref[...] = jnp.dot(edge, ik_scr[...], preferred_element_type=F32).astype(BF16)
    acc_t[...] += jnp.dot(iq.T, edge, preferred_element_type=F32)

    @pl.when(c == n_ctx - 1)
    def _():
        acc[...] = acc_t[...].T.astype(BF16)
        number = meta[samples * listed + s]
        for at in range(near):
            shard = me if at == 0 else (me - at if at < n_ctx else me + (at - n_ctx + 1))
            first, many = span(meta, s * listed, listed, number, shard, per_shard)

            def emit(j, _, out=outs[at], first=first):
                out[pl.ds(pl.multiple_of(j * BLK, BLK), BLK), :] = acc[
                    pl.ds(pl.multiple_of((first + j) * BLK, BLK), BLK), :
                ]
                return 0

            lax.fori_loop(0, many, emit, 0)


def indexer(meta, idx_query, wcol, ikeys, grads, dims, n_ctx):
    samples, listed, slots, per_shard, width, tiles = dims
    total, ind = idx_query.shape[1:]
    part, keys = grads[0].shape[1:]
    groups = total // (part * n_ctx)
    near = 2 * n_ctx - 1
    chunk = part * groups

    def rows(columns):
        return pl.BlockSpec((None, chunk, columns), lambda s, c: (s, c, 0))

    def whole(shape):
        return pl.BlockSpec(shape, lambda s, c: (0,) * len(shape))

    slot_rows = slots * BLK
    out = pl.pallas_call(
        functools.partial(indexer_kernel, dims, n_ctx, groups),
        grid=(samples, n_ctx),
        out_shape=[
            jax.ShapeDtypeStruct(idx_query.shape, BF16),
            jax.ShapeDtypeStruct((samples, total, 1), F32),
        ]
        + [jax.ShapeDtypeStruct((samples, slot_rows, ind), BF16)] * near,
        in_specs=[smem_spec(), rows(ind), rows(1)]
        + [whole((keys, ind))] * samples
        + [whole(grads[0].shape)] * n_ctx,
        out_specs=[rows(ind), rows(1)]
        + [pl.BlockSpec((None, slot_rows, ind), lambda s, c: (s, 0, 0))] * near,
        scratch_shapes=[
            pltpu.VMEM((n_ctx, part, keys), F32),
            pltpu.VMEM((keys, ind), BF16),
            pltpu.VMEM((ind, keys), F32),
            pltpu.VMEM((keys, ind), BF16),
        ],
        compiler_params=params(),
        cost_estimate=cost(6 * samples * total * keys * ind, 8 * samples * total * LANE * 2),
        name="indexer",
    )(meta, idx_query, wcol, *ikeys, *grads)
    return out[0], out[1], out[2:]


def settle_kernel(dims, n_smp, here, *refs):
    samples, listed, slots, per_shard, width, tiles = dims
    slabs = refs[: n_smp * samples]
    iks = refs[n_smp * samples : n_smp * (samples + 1)]
    out_kv, out_ik, acc, acc_i = refs[n_smp * (samples + 1) :]
    each = samples * (listed + 1)
    me = here[n_smp * each]
    place = here[n_smp * each + 1]
    mine = per_shard // n_smp
    base = me * per_shard + place * mine
    value = tiles * LANE
    acc[...] = jnp.zeros_like(acc)
    acc_i[...] = jnp.zeros_like(acc_i)
    for at in range(n_smp):
        chips = n_smp // 2
        core, chip = at // chips, at % chips
        source = lax.rem((place ^ core) - 2 * chip + n_smp, n_smp)
        for s in range(samples):
            start = source * each + s * listed
            number = here[source * each + samples * listed + s]
            shard_first, _ = span(here, start, listed, number, me, per_shard)
            first = below(here, start, listed, number, base)
            last = below(here, start, listed, number, base + mine)

            def add(i, _, slab=slabs[at * samples + s], ik=iks[at], s=s, start=start, zero=shard_first):
                j = i - zero
                to = pl.multiple_of((here[start + i] - base) * BLK, BLK)
                rows = pl.ds(to, BLK)
                for c in range(tiles):
                    acc[rows, c * LANE : (c + 1) * LANE] += slab[
                        pl.ds(pl.multiple_of((c * slots + j) * BLK, BLK), BLK), :
                    ].astype(F32)
                tail = slab[
                    pl.ds(pl.multiple_of(tiles * slots * BLK + j * HALF, HALF), HALF), :
                ].astype(F32)
                side = LANE // 2
                acc[pl.ds(to, HALF), value : value + side] += tail[:, :side]
                acc[pl.ds(pl.multiple_of(to + HALF, HALF), HALF), value : value + side] += tail[
                    :, side:
                ]
                acc_i[rows, :] += ik[s, pl.ds(pl.multiple_of(j * BLK, BLK), BLK), :].astype(F32)
                return 0

            lax.fori_loop(first, last, add, 0)
    out_kv[...] = acc[:, :width].astype(BF16)
    out_ik[...] = acc_i[...].astype(BF16)


def settle(here, slabs, iks, dims, n_smp):
    samples, listed, slots, per_shard, width, tiles = dims
    rows = per_shard * BLK // n_smp
    ind = iks[0].shape[2]
    wide = (width + LANE - 1) // LANE * LANE
    return pl.pallas_call(
        functools.partial(settle_kernel, dims, n_smp),
        out_shape=[
            jax.ShapeDtypeStruct((rows, width), BF16),
            jax.ShapeDtypeStruct((rows, ind), BF16),
        ],
        in_specs=[smem_spec()] + [vmem_spec()] * (len(slabs) + len(iks)),
        out_specs=[vmem_spec()] * 2,
        scratch_shapes=[pltpu.VMEM((rows, wide), F32), pltpu.VMEM((rows, ind), F32)],
        compiler_params=params(),
        cost_estimate=cost(0, 4 * rows * width * 2),
        name="settle",
    )(here, *slabs, *iks)


def spread_blocks(own, n):
    rights, lefts = [], []
    right = left = own
    for step in range(1, n):
        right = lax.ppermute(right, "ctx", [(i, i + 1) for i in range(step - 1, n - 1)])
        left = lax.ppermute(left, "ctx", [(i, i - 1) for i in range(1, n - step + 1)])
        rights.append(right)
        lefts.append(left)
    return [own] + rights + lefts


def gather_sums(parts, n):
    before, after = parts[1:n], parts[n:]

    def add(a, b):
        return (a.astype(F32) + b.astype(F32)).astype(BF16)

    left, right = before[n - 2], after[n - 2]
    for far in range(n - 1, 0, -1):
        right = lax.ppermute(right, "ctx", [(i, i + 1) for i in range(n - far)])
        left = lax.ppermute(left, "ctx", [(i, i - 1) for i in range(far, n)])
        if far > 1:
            right = add(right, after[far - 2])
            left = add(left, before[far - 2])
    return (parts[0].astype(F32) + right.astype(F32) + left.astype(F32)).astype(BF16)


def shifted(x, axis, n, by):
    return lax.ppermute(x, axis, [(i, (i + by) % n) for i in range(n)])


def exchange(x, n):
    chips = [x] + [shifted(x, "smp", n, 2 * k) for k in range(1, n // 2)]
    other = [lax.ppermute(y, "smp", [(i, i ^ 1) for i in range(n)]) for y in chips]
    return chips + other


def shards(kv, idx_key, query, dout, idx_query, idx_weight, blocks, counts):
    n_ctx = lax.axis_size("ctx")
    n_smp = lax.axis_size("smp")
    me = lax.axis_index("ctx").astype(jnp.int32)
    place = lax.axis_index("smp").astype(jnp.int32)
    samples, listed = blocks.shape
    width = kv.shape[1]
    value = dout.shape[3]
    _, every, heads, _ = query.shape
    groups = idx_query.shape[2]
    dims = (
        samples,
        listed,
        max(2, 2 * listed // n_ctx),
        kv.shape[0] // BLK,
        width,
        value // LANE,
    )
    lists = jnp.concatenate([blocks.reshape(-1), counts])
    meta = jnp.concatenate([lists, me[None]])
    here = jnp.concatenate(
        [lax.all_gather(lists, "smp").reshape(-1), jnp.stack([me, place])]
    )
    q = query.reshape(samples, every * heads, width)
    do = dout.reshape(samples, every * heads, value)
    iq = idx_query.reshape(samples, every * groups, idx_query.shape[3])
    wcol = idx_weight.astype(F32).reshape(samples, every * groups, 1)
    tall = min(256, every * heads)

    slabs = [spread_blocks(own, n_ctx) for own in pack(meta, kv, idx_key, dims)]
    d_query = None
    ikeys, sums, pieces = [], [], []
    for s in range(samples):
        d_query, ikey, grads, parts = attention(
            meta, q, do, iq, wcol, slabs[s], d_query, dims, s, n_ctx, heads, tall
        )
        ikeys.append(ikey)
        pieces += [parts[0]] + [shifted(parts[k], "ctx", n_ctx, k) for k in range(1, n_ctx)]
        sums.append(gather_sums(grads, n_ctx))
    grad = divergence(meta, pieces, samples, listed, n_ctx)
    grads = [grad] + [shifted(grad, "ctx", n_ctx, k) for k in range(1, n_ctx)]
    d_idx_query, d_weight, parts = indexer(meta, iq, wcol, ikeys, grads, dims, n_ctx)
    iks = exchange(gather_sums(parts, n_ctx), n_smp)
    exchanged = [exchange(x, n_smp) for x in sums]
    out_kv, out_ik = settle(
        here, [exchanged[s][at] for at in range(n_smp) for s in range(samples)], iks, dims, n_smp
    )
    return (
        d_query.reshape(query.shape),
        d_idx_query.reshape(idx_query.shape),
        d_weight.reshape(idx_weight.shape).astype(BF16),
        out_kv,
        out_ik,
    )


def solution(mesh):
    return jax.shard_map(
        shards,
        mesh=mesh,
        in_specs=(
            P(("rep", "ctx"), None),
            P(("rep", "ctx"), None),
            P(("rep", "smp"), None, "ctx", None),
            P(("rep", "smp"), None, "ctx", None),
            P(("rep", "smp"), None, "ctx", None),
            P(("rep", "smp"), None, "ctx"),
            P(("rep", "smp"), None),
            P(("rep", "smp")),
        ),
        out_specs=(
            P(("rep", "smp"), None, "ctx", None),
            P(("rep", "smp"), None, "ctx", None),
            P(("rep", "smp"), None, "ctx"),
            P(("rep", "ctx", "smp"), None),
            P(("rep", "ctx", "smp"), None),
        ),
        check_vma=False,
    )
```

```python
import functools

import jax
import jax.numpy as jnp
from jax import lax
from jax.experimental import pallas as pl
from jax.experimental.pallas import tpu as pltpu
from jax.sharding import PartitionSpec as P

H = 128
BLK = 64
HALF = BLK // 2
LANE = 128

SCALE = 192.0 ** (-0.5)
IDX_SCALE = 128.0 ** (-0.5)
LOSS = 256.0
NEG = -1e30
EXACT = lax.Precision.HIGHEST
VMEM_BYTES = 56 * 1024 * 1024

NT = (((1,), (1,)), ((), ()))
F32 = jnp.float32
BF16 = jnp.bfloat16


def params():
    return pltpu.CompilerParams(vmem_limit_bytes=VMEM_BYTES)


def cost(flops, moved):
    return pl.CostEstimate(flops=int(flops), bytes_accessed=int(moved), transcendentals=0)


def any_spec():
    return pl.BlockSpec(memory_space=pl.ANY)


def vmem_spec():
    return pl.BlockSpec(memory_space=pltpu.VMEM)


def smem_spec():
    return pl.BlockSpec(memory_space=pltpu.SMEM)


def below(meta, base, listed, number, bound):
    total = jnp.int32(0)
    for i in range(listed):
        total += jnp.where((i < number) & (meta[base + i] < bound), 1, 0)
    return total


def span(meta, base, listed, number, shard, per_shard):
    first = below(meta, base, listed, number, shard * per_shard)
    last = below(meta, base, listed, number, (shard + 1) * per_shard)
    return first, last - first


def pack_kernel(dims, meta, kv_t, ik, *rest):
    samples, listed, slots, per_shard, width, tiles = dims
    outs, (kbuf, ibuf, sem) = rest[:samples], rest[samples:]
    me = meta[samples * (listed + 1)]
    copies, sides = [], []
    for s in range(samples):
        number = meta[samples * listed + s]
        first, _ = span(meta, s * listed, listed, number, me, per_shard)
        for j in range(slots):
            at = s * slots + j
            place = jnp.minimum(first + j, listed - 1)
            block = jnp.clip(meta[s * listed + place] - me * per_shard, 0, per_shard - 1)
            rows = pl.ds(pl.multiple_of(block * BLK, BLK), BLK)
            pair = pl.ds(pl.multiple_of(block // 2 * LANE, LANE), LANE)
            one = pltpu.make_async_copy(kv_t.at[:, pair], kbuf.at[at], sem.at[at, 0])
            two = pltpu.make_async_copy(ik.at[rows], ibuf.at[at], sem.at[at, 1])
            one.start()
            two.start()
            copies.append((one, two))
            sides.append(lax.rem(block, 2) == 0)
    for at in range(samples * slots):
        out, j = outs[at // slots], at % slots
        copies[at][0].wait()
        copies[at][1].wait()
        for c in range(tiles):
            both = kbuf[at, c * LANE : (c + 1) * LANE, :].T
            out[pl.ds((c * slots + j) * BLK, BLK), :] = jnp.where(sides[at], both[:BLK], both[BLK:])
        out[pl.ds((tiles * slots + j) * BLK, BLK), :] = ibuf[at]
        both = kbuf[at, tiles * LANE : width, :].T
        tail = jnp.where(sides[at], both[:BLK], both[BLK:])
        out[pl.ds((tiles + 1) * slots * BLK + j * HALF, HALF), :] = jnp.concatenate(
            [tail[:HALF], tail[HALF:]], axis=1
        )


def pack(meta, kv_t, ik, dims):
    samples, listed, slots, per_shard, width, tiles = dims
    rows = slots * ((tiles + 1) * BLK + HALF)
    return pl.pallas_call(
        functools.partial(pack_kernel, dims),
        out_shape=[jax.ShapeDtypeStruct((rows, LANE), BF16)] * samples,
        in_specs=[smem_spec(), any_spec(), any_spec()],
        out_specs=[vmem_spec()] * samples,
        scratch_shapes=[
            pltpu.VMEM((samples * slots, width, LANE), BF16),
            pltpu.VMEM((samples * slots, BLK, ik.shape[1]), BF16),
            pltpu.SemaphoreType.DMA((samples * slots, 2)),
        ],
        compiler_params=params(),
        cost_estimate=cost(0, 4 * samples * rows * LANE * 2),
        name="pack",
    )(meta, kv_t, ik)


def shard_of(at, me, n_ctx):
    if at == 0:
        return me
    return me - at if at < n_ctx else me + (at - n_ctx + 1)


def unpack_slab(slab, first, many, slots, tiles, k_ref, ikey_ref):
    value, side = tiles * LANE, LANE // 2

    def place(j, _):
        to = pl.multiple_of((first + j) * BLK, BLK)
        for c in range(tiles + 1):
            piece = slab[pl.ds(pl.multiple_of((c * slots + j) * BLK, BLK), BLK), :]
            if c < tiles:
                k_ref[pl.ds(to, BLK), c * LANE : (c + 1) * LANE] = piece
            else:
                ikey_ref[pl.ds(to, BLK), :] = piece
        piece = slab[pl.ds(pl.multiple_of((tiles + 1) * slots * BLK + j * HALF, HALF), HALF), :]
        k_ref[pl.ds(to, HALF), value : value + side] = piece[:, :side]
        k_ref[pl.ds(pl.multiple_of(to + HALF, HALF), HALF), value : value + side] = piece[:, side:]
        return 0

    lax.fori_loop(0, many, place, 0)


def emit_slab(acc, out, first, many, slots, tiles):
    value, side = tiles * LANE, LANE // 2

    def emit(j, _):
        rows = pl.ds(pl.multiple_of((first + j) * BLK, BLK), BLK)
        for c in range(tiles):
            out[pl.ds(pl.multiple_of((c * slots + j) * BLK, BLK), BLK), :] = acc[
                rows, c * LANE : (c + 1) * LANE
            ].astype(BF16)
        tail = acc[rows, value : value + side].astype(BF16)
        out[pl.ds(pl.multiple_of(tiles * slots * BLK + j * HALF, HALF), HALF), :] = (
            jnp.concatenate([tail[:HALF], tail[HALF:]], axis=1)
        )
        return 0

    lax.fori_loop(0, many, emit, 0)


def attention_kernel(dims, s, n_ctx, heads, groups, lo, opens, closes, riding, extra, meta, *refs):
    samples, listed, slots, per_shard, width, tiles = dims
    near = 2 * n_ctx - 1
    refs = list(refs)

    def take(count):
        head = refs[:count]
        del refs[:count]
        return head

    q_ref, do_ref, iq_ref, wcol_ref = take(4)
    slabs = take(near) if opens else []
    carried = [] if opens else take(6)
    riders = take(riding)
    take(extra)
    (dq_ref,) = take(1)
    if closes:
        outs, parts = take(near), take(n_ctx)
    if opens:
        ikey_ref, k_ref, kt_ref, acc, mass_t, logits = take(6)
    else:
        ikey_ref, k_ref, kt_ref = carried[:3]
        acc, mass_t, logits = take(3)
    step = pl.program_id(0)
    value = tiles * LANE
    keys = listed * BLK
    rows = q_ref.shape[0]
    times = rows // heads
    every = mass_t.shape[1]
    me = meta[samples * (listed + 1)]
    number = meta[samples * listed + s]
    live = number * BLK

    @pl.when(step == 0)
    def _():
        if not opens:
            acc[...] = carried[3][...]
            mass_t[...] = carried[4][...]
            logits[...] = carried[5][...]
            return
        for at in range(near):
            first, many = span(
                meta, s * listed, listed, number, shard_of(at, me, n_ctx), per_shard
            )
            unpack_slab(slabs[at], first, many, slots, tiles, k_ref, ikey_ref)

        def clear(i, _):
            to = pl.multiple_of(i * BLK, BLK)
            k_ref[pl.ds(to, BLK), :] = jnp.zeros((BLK, k_ref.shape[1]), BF16)
            ikey_ref[pl.ds(to, BLK), :] = jnp.zeros((BLK, ikey_ref.shape[1]), BF16)
            return 0

        lax.fori_loop(number, listed, clear, 0)
        k_ref[:, width:] = jnp.zeros((keys, k_ref.shape[1] - width), BF16)
        kt_ref[...] = k_ref[...].T
        acc[...] = jnp.zeros_like(acc)
        mass_t[...] = jnp.zeros_like(mass_t)
        logits[...] = jnp.zeros_like(logits)

    q = q_ref[...]
    do = do_ref[...]
    scores = lax.dot_general(k_ref[:, :width], q, NT, preferred_element_type=F32)
    alive = lax.broadcasted_iota(jnp.int32, (keys, 1), 0) < live
    scores = jnp.where(alive, scores * SCALE, NEG)
    expo = jnp.exp(scores - jnp.max(scores, axis=0, keepdims=True))
    probs = expo * (1.0 / jnp.sum(expo, axis=0, keepdims=True))
    probs_b = probs.astype(BF16)
    dprob = lax.dot_general(k_ref[:, :value], do, NT, preferred_element_type=F32)
    delta = jnp.sum(probs * dprob, axis=0, keepdims=True)
    dscore = (probs * (dprob - delta) * SCALE).astype(BF16)
    dq_t = jnp.dot(kt_ref[...], dscore, preferred_element_type=F32)
    dq_ref[...] = dq_t.T[:, :width].astype(BF16)
    acc[:, :width] += jnp.dot(dscore, q, preferred_element_type=F32)
    acc[:, :value] += jnp.dot(probs_b, do, preferred_element_type=F32)
    row = lax.broadcasted_iota(jnp.int32, (rows, every), 0) // heads + (lo + step) * times
    column = lax.broadcasted_iota(jnp.int32, (rows, every), 1)
    member = jnp.where(row == column, 1.0, 0.0).astype(BF16)
    mass_t[...] += jnp.dot(probs_b, member, preferred_element_type=F32)

    inner = lax.dot_general(iq_ref[...], ikey_ref[...], NT, preferred_element_type=F32)
    weighed = jnp.maximum(inner, 0.0) * (wcol_ref[...] * IDX_SCALE)
    if groups % 8 == 0:
        logit = jnp.sum(weighed.reshape(times, groups, keys), axis=1)
    else:
        fold = (
            lax.broadcasted_iota(jnp.int32, (times, times * groups), 1) // groups
            == lax.broadcasted_iota(jnp.int32, (times, times * groups), 0)
        ).astype(F32)
        logit = jnp.dot(fold, weighed, precision=EXACT, preferred_element_type=F32)
    logits[pl.ds(pl.multiple_of((lo + step) * times, times), times), :] = logit

    if closes:

        @pl.when(step == pl.num_programs(0) - 1)
        def _():
            for at in range(near):
                first, many = span(
                    meta, s * listed, listed, number, shard_of(at, me, n_ctx), per_shard
                )
                emit_slab(acc, outs[at], first, many, slots, tiles)
            mass = mass_t[...].T
            part = every // n_ctx
            behind = riders[0].shape[0] if riding else 0
            for k in range(riding):
                parts[k][:behind] = riders[k][...]
            for c in range(n_ctx):
                to = lax.rem(c - me + n_ctx, n_ctx)
                here = slice(c * part, (c + 1) * part)
                for k in range(n_ctx):

                    @pl.when(to == k)
                    def _(here=here, k=k):
                        parts[k][behind : behind + part] = mass[here]
                        parts[k][behind + part :] = logits[here, :]


def attention(meta, query, dout, idx_query, wcol, slabs, state, riders, d_query, dims, s, n_ctx,
              heads, tall, lo, hi, after):
    samples, listed, slots, per_shard, width, tiles = dims
    total = query.shape[1]
    every = total // heads
    groups = idx_query.shape[1] // every
    ind = idx_query.shape[2]
    side = tall // heads * groups
    value = tiles * LANE
    keys = listed * BLK
    wide = (width + LANE - 1) // LANE * LANE
    near = 2 * n_ctx - 1
    opens, closes = lo == 0, hi == total // tall
    grad_rows = slots * (tiles * BLK + HALF)

    def row_spec(size, columns):
        return pl.BlockSpec((None, size, columns), lambda i: (s, lo + i, 0))

    def whole(shape):
        return pl.BlockSpec(shape, lambda i: (0,) * len(shape))

    args = [meta, query, dout, idx_query, wcol]
    in_specs = [
        smem_spec(), row_spec(tall, width), row_spec(tall, value), row_spec(side, ind),
        row_spec(side, 1),
    ]
    if opens:
        args += slabs
        in_specs += [whole(slabs[0].shape)] * near
    else:
        args += state
        in_specs += [whole(x.shape) for x in state]
    args += riders
    in_specs += [whole(x.shape) for x in riders]
    aliases = {}
    if d_query is not None:
        aliases = {len(args): 0}
        args.append(d_query)
        in_specs.append(any_spec())
    args += after
    in_specs += [any_spec()] * len(after)
    store = [
        ((keys, ind), BF16), ((keys, wide), BF16), ((wide, keys), BF16), ((keys, wide), F32),
        ((keys, every), F32), ((every, keys), F32),
    ]
    out_shape = [(query.shape, BF16)]
    out_specs = [row_spec(tall, width)]
    scratch = []
    if closes:
        out_shape += [((grad_rows, LANE), BF16)] * near
        behind = riders[0].shape[0] if riders else 0
        out_shape += [((behind + 2 * (every // n_ctx), keys), F32)] * n_ctx
    kept = len(out_shape)
    if opens:
        out_shape += store[:1] if closes else store
    if closes:
        scratch = [pltpu.VMEM(*x) for x in (store[1:] if opens else store[3:])]
    out_specs += [whole(x[0]) for x in out_shape[1:]]
    count = (hi - lo) * tall
    out = pl.pallas_call(
        functools.partial(
            attention_kernel, dims, s, n_ctx, heads, groups, lo, opens, closes,
            len(riders), len(aliases) + len(after),
        ),
        grid=(hi - lo,),
        out_shape=[jax.ShapeDtypeStruct(*x) for x in out_shape],
        in_specs=in_specs,
        out_specs=out_specs,
        scratch_shapes=scratch,
        input_output_aliases=aliases,
        compiler_params=params(),
        cost_estimate=cost(
            2 * count * keys * (3 * width + 2 * value),
            count * (2 * width + value) * 2 + 14 * grad_rows * LANE * 2,
        ),
        name="attention",
    )(*args)
    if not closes:
        return out[0], list(out[1:])
    ikey = out[kept] if opens else state[0]
    return out[0], list(out[1 : 1 + near]), list(out[1 + near : kept]), ikey


def divergence_kernel(samples, listed, n_ctx, meta, *refs):
    out = refs[-1]
    part, keys = out.shape[1:]
    total = refs[0][...]
    for k in range(1, n_ctx):
        total += refs[k][...]
    for s in range(samples):
        mass = total[2 * s * part : (2 * s + 1) * part]
        alive = lax.broadcasted_iota(jnp.int32, (1, keys), 1) < meta[samples * listed + s] * BLK
        logit = jnp.where(alive, total[(2 * s + 1) * part : (2 * s + 2) * part], NEG)
        expo = jnp.exp(logit - jnp.max(logit, axis=1, keepdims=True))
        share = expo / jnp.sum(expo, axis=1, keepdims=True)
        out[s] = LOSS * (share - mass * (1.0 / H))


def divergence(meta, pieces, samples, listed, n_ctx, after):
    rows, keys = pieces[0].shape
    return pl.pallas_call(
        functools.partial(divergence_kernel, samples, listed, n_ctx),
        out_shape=jax.ShapeDtypeStruct((samples, rows // samples // 2, keys), F32),
        in_specs=[smem_spec()] + [vmem_spec()] * n_ctx + [any_spec()] * len(after),
        out_specs=vmem_spec(),
        compiler_params=params(),
        cost_estimate=cost(0, n_ctx * rows * keys * 4),
        name="divergence",
    )(meta, *pieces, *after)


def indexer_kernel(dims, n_ctx, groups, extra, meta, *refs):
    samples, listed, slots, per_shard, width, tiles = dims
    near = 2 * n_ctx - 1
    iq_ref, wcol_ref = refs[:2]
    ikeys = refs[2 : 2 + samples]
    grads = refs[2 + samples : 2 + samples + n_ctx]
    refs = refs[2 + samples + n_ctx + extra :]
    diq_ref, dw_ref = refs[:2]
    outs = refs[2 : 2 + near]
    whole, ik_scr, acc_t, acc = refs[2 + near :]
    s, c = pl.program_id(0), pl.program_id(1)
    me = meta[samples * (listed + 1)]
    part, keys = grads[0].shape[1:]

    @pl.when(c == 0)
    def _():
        for k in range(n_ctx):
            whole[lax.rem(me - k + n_ctx, n_ctx)] = grads[k][s]
        for at in range(samples):

            @pl.when(s == at)
            def _(at=at):
                ik_scr[...] = ikeys[at][...]

        acc_t[...] = jnp.zeros_like(acc_t)

    iq = iq_ref[...]
    inner = lax.dot_general(iq, ik_scr[...], NT, preferred_element_type=F32)
    grad = whole[c]
    if groups % 8 == 0:
        grad = jnp.broadcast_to(grad[:, None, :], (part, groups, keys)).reshape(part * groups, keys)
    else:
        expand = (
            lax.broadcasted_iota(jnp.int32, (part * groups, part), 0) // groups
            == lax.broadcasted_iota(jnp.int32, (part * groups, part), 1)
        ).astype(F32)
        grad = jnp.dot(expand, grad, precision=EXACT, preferred_element_type=F32)
    edge = jnp.where(inner > 0.0, grad * (wcol_ref[...] * IDX_SCALE), 0.0).astype(BF16)
    dw_ref[...] = jnp.sum(grad * jnp.maximum(inner, 0.0), axis=1, keepdims=True) * IDX_SCALE
    diq_ref[...] = jnp.dot(edge, ik_scr[...], preferred_element_type=F32).astype(BF16)
    acc_t[...] += jnp.dot(iq.T, edge, preferred_element_type=F32)

    @pl.when(c == n_ctx - 1)
    def _():
        acc[...] = acc_t[...].T.astype(BF16)
        number = meta[samples * listed + s]
        for at in range(near):
            shard = shard_of(at, me, n_ctx)
            first, many = span(meta, s * listed, listed, number, shard, per_shard)

            def emit(j, _, out=outs[at], first=first):
                out[pl.ds(pl.multiple_of(j * BLK, BLK), BLK), :] = acc[
                    pl.ds(pl.multiple_of((first + j) * BLK, BLK), BLK), :
                ]
                return 0

            lax.fori_loop(0, many, emit, 0)


def indexer(meta, idx_query, wcol, ikeys, grads, dims, n_ctx, after):
    samples, listed, slots, per_shard, width, tiles = dims
    total, ind = idx_query.shape[1:]
    part, keys = grads[0].shape[1:]
    groups = total // (part * n_ctx)
    near = 2 * n_ctx - 1
    chunk = part * groups

    def rows(columns):
        return pl.BlockSpec((None, chunk, columns), lambda s, c: (s, c, 0))

    def whole(shape):
        return pl.BlockSpec(shape, lambda s, c: (0,) * len(shape))

    slot_rows = slots * BLK
    out = pl.pallas_call(
        functools.partial(indexer_kernel, dims, n_ctx, groups, len(after)),
        grid=(samples, n_ctx),
        out_shape=[
            jax.ShapeDtypeStruct(idx_query.shape, BF16),
            jax.ShapeDtypeStruct((samples, total, 1), F32),
        ]
        + [jax.ShapeDtypeStruct((samples, slot_rows, ind), BF16)] * near,
        in_specs=[smem_spec(), rows(ind), rows(1)]
        + [whole((keys, ind))] * samples
        + [whole(grads[0].shape)] * n_ctx
        + [any_spec()] * len(after),
        out_specs=[rows(ind), rows(1)]
        + [pl.BlockSpec((None, slot_rows, ind), lambda s, c: (s, 0, 0))] * near,
        scratch_shapes=[
            pltpu.VMEM((n_ctx, part, keys), F32),
            pltpu.VMEM((keys, ind), BF16),
            pltpu.VMEM((ind, keys), F32),
            pltpu.VMEM((keys, ind), BF16),
        ],
        compiler_params=params(),
        cost_estimate=cost(6 * samples * total * keys * ind, 8 * samples * total * LANE * 2),
        name="indexer",
    )(meta, idx_query, wcol, *ikeys, *grads, *after)
    return out[0], out[1], out[2:]


def settle_kernel(dims, n_smp, here, *refs):
    samples, listed, slots, per_shard, width, tiles = dims
    slabs = refs[: n_smp * samples]
    lasts = refs[n_smp * samples : n_smp * (samples + 1)]
    out_kv, out_ik, acc, acc_i = refs[n_smp * (samples + 1) :]
    each = samples * (listed + 1)
    me = here[n_smp * each]
    place = here[n_smp * each + 1]
    mine = per_shard // n_smp
    base = me * per_shard + place * mine
    value = tiles * LANE
    acc[...] = jnp.zeros_like(acc)
    acc_i[...] = jnp.zeros_like(acc_i)
    for at in range(n_smp):
        for s in range(samples):
            start = at * each + s * listed
            number = here[at * each + samples * listed + s]
            shard_first, _ = span(here, start, listed, number, me, per_shard)
            first = below(here, start, listed, number, base)
            last = below(here, start, listed, number, base + mine)

            skip = s * slots * BLK

            def add(
                i, _, slab=slabs[at * samples + s], ik=lasts[at], skip=skip, start=start,
                zero=shard_first,
            ):
                j = i - zero
                to = pl.multiple_of((here[start + i] - base) * BLK, BLK)
                rows = pl.ds(to, BLK)
                for c in range(tiles):
                    acc[rows, c * LANE : (c + 1) * LANE] += slab[
                        pl.ds(pl.multiple_of((c * slots + j) * BLK, BLK), BLK), :
                    ].astype(F32)
                tail = slab[
                    pl.ds(pl.multiple_of(tiles * slots * BLK + j * HALF, HALF), HALF), :
                ].astype(F32)
                side = LANE // 2
                acc[pl.ds(to, HALF), value : value + side] += tail[:, :side]
                acc[pl.ds(pl.multiple_of(to + HALF, HALF), HALF), value : value + side] += tail[
                    :, side:
                ]
                acc_i[rows, :] += ik[pl.ds(pl.multiple_of(skip + j * BLK, BLK), BLK), :].astype(F32)
                return 0

            lax.fori_loop(first, last, add, 0)
    for c in range(acc.shape[0] // LANE):
        rows = slice(c * LANE, (c + 1) * LANE)
        out_kv[:, rows] = acc[rows, :].astype(BF16).T[:width]
    out_ik[...] = acc_i[...].astype(BF16)


def settle(here, slabs, lasts, dims, n_smp):
    samples, listed, slots, per_shard, width, tiles = dims
    rows = per_shard * BLK // n_smp
    ind = lasts[0].shape[1]
    wide = (width + LANE - 1) // LANE * LANE
    return pl.pallas_call(
        functools.partial(settle_kernel, dims, n_smp),
        out_shape=[
            jax.ShapeDtypeStruct((width, rows), BF16),
            jax.ShapeDtypeStruct((rows, ind), BF16),
        ],
        in_specs=[smem_spec()] + [vmem_spec()] * (len(slabs) + len(lasts)),
        out_specs=[vmem_spec()] * 2,
        scratch_shapes=[pltpu.VMEM((rows, wide), F32), pltpu.VMEM((rows, ind), F32)],
        compiler_params=params(),
        cost_estimate=cost(0, 4 * rows * width * 2),
        name="settle",
    )(here, *slabs, *lasts)


def spread_blocks(own, n, holds=()):
    rights, lefts = [], []
    right = left = own
    for step in range(1, n):
        hold = holds[step - 1] if step <= len(holds) else []
        if hold and step == 1:
            right = left = tie([own], hold)[0]
        elif hold:
            right, left = tie([right, left], hold)
        right = lax.ppermute(right, "ctx", [(i, i + 1) for i in range(step - 1, n - 1)])
        left = lax.ppermute(left, "ctx", [(i, i - 1) for i in range(1, n - step + 1)])
        rights.append(right)
        lefts.append(left)
    return [own] + rights + lefts


def add(a, b):
    return (a.astype(F32) + b.astype(F32)).astype(BF16)


class Sums:
    def __init__(self, parts, n):
        self.own, self.before, self.later, self.n = parts[0], parts[1:n], parts[n:], n
        self.came = []

    def step(self, hold=()):
        far = self.n - 1 - len(self.came)
        left, right = self.before[far - 1], self.later[far - 1]
        if self.came:
            right, left = add(self.came[-1][0], right), add(self.came[-1][1], left)
        if hold:
            left, right = tie([left, right], list(hold))
        right = lax.ppermute(right, "ctx", [(i, i + 1) for i in range(self.n - far)])
        left = lax.ppermute(left, "ctx", [(i, i - 1) for i in range(far, self.n)])
        self.came.append([right, left])
        return self.came[-1]

    def total(self):
        right, left = self.came[-1]
        return (self.own.astype(F32) + right.astype(F32) + left.astype(F32)).astype(BF16)


def tie_kernel(*refs):
    pass


def tie(arrays, after):
    count = len(arrays)
    return list(
        pl.pallas_call(
            tie_kernel,
            out_shape=[jax.ShapeDtypeStruct(x.shape, x.dtype) for x in arrays],
            in_specs=[any_spec()] * (count + len(after)),
            out_specs=[any_spec()] * count,
            input_output_aliases={i: i for i in range(count)},
            compiler_params=params(),
            cost_estimate=cost(0, 0),
            name="tie",
        )(*arrays, *after)
    )


def shifted(x, axis, n, by):
    return lax.ppermute(x, axis, [(i, (i + by) % n) for i in range(n)])


def exchange(x, n):
    chips = [x] + [shifted(x, "smp", n, 2 * k) for k in range(1, n // 2)]
    other = [lax.ppermute(y, "smp", [(i, i ^ 1) for i in range(n)]) for y in chips]
    return chips + other


def shards(kv, idx_key, query, dout, idx_query, idx_weight, blocks, counts):
    n_ctx = lax.axis_size("ctx")
    n_smp = lax.axis_size("smp")
    me = lax.axis_index("ctx").astype(jnp.int32)
    place = lax.axis_index("smp").astype(jnp.int32)
    samples, listed = blocks.shape
    width = kv.shape[1]
    value = dout.shape[3]
    _, every, heads, _ = query.shape
    groups = idx_query.shape[2]
    dims = (
        samples,
        listed,
        max(2, 2 * listed // n_ctx),
        kv.shape[0] // BLK,
        width,
        value // LANE,
    )
    lists = jnp.concatenate([blocks.reshape(-1), counts])
    meta = jnp.concatenate([lists, me[None]])
    here = jnp.concatenate(exchange(lists, n_smp) + [jnp.stack([me, place])])
    q = query.reshape(samples, every * heads, width)
    do = dout.reshape(samples, every * heads, value)
    iq = idx_query.reshape(samples, every * groups, idx_query.shape[3])
    wcol = idx_weight.astype(F32).reshape(samples, every * groups, 1)
    tall = min(512, every * heads)
    steps = every * heads // tall

    packed = pack(meta, kv.T, idx_key, dims)
    slabs = [spread_blocks(packed[0], n_ctx)]
    d_query = None
    ikeys, parts, rings = [], [], []
    for s in range(samples):
        more = s + 1 < samples
        cut = steps // 2 if samples > 1 and steps > 1 else 0
        state, carry, ready = [], [], rings[-1].came[0] if rings else []
        if cut:
            d_query, state = attention(
                meta, q, do, iq, wcol, slabs[s], [], [], d_query, dims, s, n_ctx, heads, tall,
                0, cut, ready,
            )
            carry, ready = state[:1], []
        if more:
            before = slabs[s]
            coming = spread_blocks(
                packed[s + 1], n_ctx, [[before[n_ctx - 1], before[-1], here], state[:1]]
            )
            ring = [[coming[k], coming[k + n_ctx - 1]] for k in range(1, n_ctx)]
            slabs.append(coming)
            ready = ring[0]
        elif cut:
            ready = rings[0].came[1 % len(rings[0].came)]
        d_query, grads, parts, ikey = attention(
            meta, q, do, iq, wcol, slabs[s], state, parts, d_query, dims, s, n_ctx, heads, tall,
            cut, steps, ready,
        )
        ikeys.append(ikey)
        rings.append(Sums(grads, n_ctx))
        if more:
            rings[-1].step(ring[1 % len(ring)])
            if n_ctx > 2:
                rings[-1].step()
    last = rings[-1]
    for ring in rings[:-1]:
        while len(ring.came) < n_ctx - 1:
            ring.step(carry)
    last.step(rings[0].came[-1] if samples > 1 else [])
    pieces = [parts[0]] + [shifted(parts[k], "ctx", n_ctx, k) for k in range(1, n_ctx)]
    grad = divergence(meta, pieces, samples, listed, n_ctx, last.came[0])
    grads = [grad] + [shifted(grad, "ctx", n_ctx, k) for k in range(1, n_ctx)]
    last.step([grad])
    exchanged = []
    for ring in rings[:-1]:
        exchanged.append(exchange(ring.total(), n_smp))
    d_idx_query, d_weight, parts = indexer(meta, iq, wcol, ikeys, grads, dims, n_ctx, [])
    small = Sums([x.reshape(-1, x.shape[-1]) for x in parts], n_ctx)
    small.step(last.came[-1])
    hold = [y for x in exchanged for y in x[1 : n_smp // 2]]
    while len(last.came) < n_ctx - 1:
        last.step()
        small.step(last.came[-1] + hold)
        hold = []
    small.step(hold)
    total = exchange(last.total(), n_smp)
    exchanged.append(total)
    out_kv, out_ik = settle(
        here,
        [exchanged[s][at] for at in range(n_smp) for s in range(samples)],
        exchange(small.total(), n_smp),
        dims,
        n_smp,
    )
    return (
        d_query.reshape(query.shape),
        d_idx_query.reshape(idx_query.shape),
        d_weight.reshape(idx_weight.shape).astype(BF16),
        out_kv.T,
        out_ik,
    )


def solution(mesh):
    return jax.shard_map(
        shards,
        mesh=mesh,
        in_specs=(
            P(("rep", "ctx"), None),
            P(("rep", "ctx"), None),
            P(("rep", "smp"), None, "ctx", None),
            P(("rep", "smp"), None, "ctx", None),
            P(("rep", "smp"), None, "ctx", None),
            P(("rep", "smp"), None, "ctx"),
            P(("rep", "smp"), None),
            P(("rep", "smp")),
        ),
        out_specs=(
            P(("rep", "smp"), None, "ctx", None),
            P(("rep", "smp"), None, "ctx", None),
            P(("rep", "smp"), None, "ctx"),
            P(("rep", "ctx", "smp"), None),
            P(("rep", "ctx", "smp"), None),
        ),
        check_vma=False,
    )
```
